32 devices in a mesh: section: 4 (over y, x), seq: 8 (over z, core).
Axes of the slice: x: 2, y: 2, z: 4, core: 2. Of those that a mesh axis runs over, the one named last changes fastest.
Arguments:
- features: bfloat16 [1024, 8192], P('seq', 'section'), may hold values from -600 to 600
- norm_gain: float32 [8192], P('section'), may hold values from 0.1 to 1.9
- kv_weight: bfloat16 [8192, 2048], P('section'), may hold values from -0.09375 to 0.09375
- queries: bfloat16 [3, 64, 1024, 128], P(None, 'section', 'seq'), may hold values from -64 to 64
- step_kv: bfloat16 [3, 8, 1024, 256], P(None, 'section', 'seq'), may hold values from -6 to 6
- doc_ids: int32 [1024], replicated, may hold values from 0 to 7, never falling along the last dimension, each value on 1 to 768 neighbouring positions
- block_lists: int32 [3, 16, 16], replicated, may hold values from 0 to 15, as said below
Outputs:
- attended: bfloat16 [3, 64, 1024, 128], P(None, 'section', 'seq')
- kv_cache: bfloat16 [8, 1024, 256], P('section', 'seq')
The draws below stay inside these ranges and needn't reach their ends.
Inputs may be any that keep to these rules, and one draw needn't show every extreme that they name: `doc_ids`: document numbers never fall along the tokens; a document holds 1 to 768 tokens, and one holds exactly 768. `block_lists`: entry [k, b, 0] is b itself; every entry of row b is at most b; entries may repeat.
All inputs are finite; a program needn't handle non-finite values.
Results may differ from the reference program's by a relative error of at most 0.0084.
Values may be sent and summed in bfloat16 or wider, within the bound.
A program may use at most 128 MiB of HBM per device.

```python
import math
import jax
import jax.numpy as jnp
import numpy as np
from jax import lax

D = 8192
HEADS = 64
KV_HEADS = 8
HEAD_DIM = 128
STEPS = 3
BLOCK = 64
LIST = 16
DOCS = 8
TOKENS = 1024
DOC_MOST = 768


def step_values(key):
    folded = jax.random.fold_in(key, 11)
    array_shape = (STEPS, KV_HEADS, TOKENS, 2 * HEAD_DIM)
    sampled = jnp.clip(jax.random.normal(folded, array_shape, jnp.float32), -6.0, 6.0)
    return sampled


def draw_step_kv(key, part):
    return step_values(key).astype(jnp.bfloat16)


def draw_queries(key, part):
    array_shape = (STEPS, HEADS, TOKENS, HEAD_DIM)
    sampled = jnp.clip(jax.random.normal(jax.random.fold_in(key, 13), array_shape, jnp.float32), -6.0, 6.0)
    result = sampled
    return result.astype(jnp.bfloat16)


def draw_features(key, part):
    column_place = jnp.arange(D, dtype=jnp.float32)[None, :] / D
    sampled = jnp.clip(jax.random.normal(jax.random.fold_in(key, 31), (TOKENS, D), jnp.float32), -4.0, 4.0)
    token_scale = 10.0 ** jax.random.uniform(jax.random.fold_in(key, 37), (TOKENS, 1), jnp.float32)
    column_scale = 10.0 ** (0.477 * column_place + 0.523 * jax.random.uniform(jax.random.fold_in(key, 41), (1, D), jnp.float32))
    return (sampled * token_scale * column_scale).astype(jnp.bfloat16)


def draw_block_lists(key, part):
    blocks = TOKENS // BLOCK
    own_block = jnp.arange(blocks, dtype=jnp.int32)[None, :, None]
    raw_draws = jax.random.randint(jax.random.fold_in(key, 23), (STEPS, blocks, LIST), 0, 1 << 20)
    candidates = raw_draws % (own_block + 1)
    slot_index = jnp.arange(LIST, dtype=jnp.int32)[None, None, :]
    return jnp.where(slot_index == 0, own_block, candidates).astype(jnp.int32)


def spiked(values, own_key, source, target, shards_of, factor):
    owner, partner = [(jnp.arange(values.shape[position]) // (values.shape[position] // shards_of)).reshape([-1 if axis == position else 1 for axis in range(values.ndim)]) for position in (source, target)]
    chosen = jax.random.permutation(own_key, shards_of)[partner]
    strong = (owner == chosen) | (owner == (partner + shards_of // 2) % shards_of)
    return jnp.where(strong, factor * values, values)


def block_scale(own_key, dims, shards, least, largest):
    gain = 1.0
    for dim, shards_of in shards:
        steps = jax.random.uniform(jax.random.fold_in(jax.random.fold_in(own_key, 6), dim), (shards_of,), jnp.float32, least / len(shards), largest / len(shards))
        gain = gain * jnp.repeat(jnp.exp(steps), dims[dim] // shards_of).reshape((-1,) + (1,) * (len(dims) - 1 - dim))
    return gain


def length_profile(number_of, total, reach, slope):
    loads = [(1 << 20) // math.isqrt(rank ** slope) + 1 for rank in range(2, number_of + 1)]
    spare, counts = total - reach - (number_of - 1), [1] * (number_of - 1)
    while spare > 0:
        free = [i for i in range(number_of - 1) if counts[i] < reach]
        mass, remaining = sum([loads[i] for i in free]), spare
        for i in free:
            extra = min(reach - counts[i], max(1, remaining * loads[i] // mass), spare)
            counts[i] = counts[i] + extra
            spare = spare - extra
    return np.array([reach] + counts)


def ragged(key, number_of, total, reach, skew):
    if number_of == 2:
        one = jax.random.randint(key, (), max(1, total - reach), min(reach, total - 1) + 1)
        return jnp.stack([one, total - one])
    lengths = jnp.asarray(length_profile(number_of, total, reach, skew), jnp.int32)
    couples = (number_of - 1) // 2
    source_of, taker = lengths[1:1 + 2 * couples:2], lengths[2:2 + 2 * couples:2]
    room = jnp.minimum(source_of - 1, reach - taker)
    shifted = jax.random.randint(jax.random.fold_in(key, 1), (couples,), 0, 1 << 20) % (room + 1)
    lengths = lengths.at[1:1 + 2 * couples:2].set(source_of - shifted).at[2:2 + 2 * couples:2].set(taker + shifted)
    return lengths[jax.random.permutation(jax.random.fold_in(key, 2), number_of)]


def bell_draw_with(own_key, shape, deviation, limit, pieces, heavy, kind=jnp.bfloat16):
    values = deviation * jax.random.normal(own_key, shape, jnp.float32)
    if pieces:
        values = values * block_scale(own_key, shape, pieces, -0.22, 0.18)
    return jnp.clip(spiked(values, jax.random.fold_in(own_key, 3), *heavy), -limit, limit).astype(kind)


def setup_inputs(seed: int = 0) -> dict:
    splits = jax.random.split(jax.random.key(seed), 8)
    return {
        "features": draw_features(jax.random.fold_in(splits[7], 71), 0),
        "norm_gain": jnp.clip(1.0 + 0.18 * jax.random.normal(splits[1], (D,), jnp.float32), 0.1, 1.9),
        "kv_weight": bell_draw_with(splits[2], (D, KV_HEADS * 2 * HEAD_DIM), D ** -0.5, 0.09375, ((0, 4),), (0, 1, 4, 2.0)),
        "queries": draw_queries(jax.random.fold_in(splits[7], 71), 0),
        "step_kv": draw_step_kv(jax.random.fold_in(splits[7], 71), 0),
        "doc_ids": jnp.searchsorted(jnp.cumsum(ragged(splits[5], DOCS, TOKENS, DOC_MOST, 2)), jnp.arange(TOKENS), side="right").astype(jnp.int32),
        "block_lists": draw_block_lists(jax.random.fold_in(splits[7], 71), 0),
    }


neg_fill = -1e+30

def reference(features, norm_gain, kv_weight, queries, step_kv, doc_ids, block_lists):
    floated = features.astype(jnp.float32)
    inverse = lax.rsqrt(lax.optimization_barrier(jnp.mean(floated * floated, axis=1, keepdims=True)) + 1e-05)
    normalized = (floated * inverse * norm_gain[None, :]).astype(jnp.bfloat16)
    weight_heads = kv_weight.reshape(D, KV_HEADS, 2 * HEAD_DIM)
    kv_cache = jnp.einsum('td,dgc->gtc', normalized.astype(jnp.float32), weight_heads.astype(jnp.float32)).astype(jnp.bfloat16)
    blocks = TOKENS // BLOCK
    group_size = HEADS // KV_HEADS
    row_span = min(512, TOKENS)
    inv_sqrt = 1.0 / math.sqrt(HEAD_DIM)
    listed = jnp.any(block_lists[..., None] == jnp.arange(blocks, dtype=jnp.int32), axis=2)
    listed_tokens = jnp.repeat(listed, BLOCK, axis=2)
    positions = jnp.arange(TOKENS, dtype=jnp.int32)
    keys_all = kv_cache[..., :HEAD_DIM].astype(jnp.float32)
    values_all = kv_cache[..., HEAD_DIM:].astype(jnp.float32)
    step_index = jnp.arange(STEPS, dtype=jnp.int32)
    own_mask = (step_index[None, :] <= step_index[:, None])[:, None, None, :]

    def one_block(block_index):
        anchor = block_index * row_span
        row_pos = anchor + jnp.arange(row_span, dtype=jnp.int32)
        row_docs = lax.dynamic_slice_in_dim(doc_ids, anchor, row_span, 0)
        row_listed = lax.dynamic_slice_in_dim(listed_tokens, anchor // BLOCK, row_span // BLOCK, 1)
        row_listed = jnp.repeat(row_listed, BLOCK, axis=1)
        allowed = row_listed & (positions[None, None, :] <= row_pos[None, :, None]) & (doc_ids[None, None, :] == row_docs[None, :, None])
        query_rows = lax.dynamic_slice_in_dim(queries, anchor, row_span, 2).astype(jnp.float32)
        grouped = jnp.moveaxis(query_rows.reshape(STEPS, KV_HEADS, group_size, row_span, HEAD_DIM), 1, 0)
        step_rows = jnp.moveaxis(lax.dynamic_slice_in_dim(step_kv, anchor, row_span, 2).astype(jnp.float32), 1, 0)

        def one_head(operands):
            head_queries, head_keys, head_values, own_rows = operands
            own_keys = own_rows[..., :HEAD_DIM]
            own_values = own_rows[..., HEAD_DIM:]
            scores = jnp.einsum('sgrd,td->sgrt', head_queries, head_keys) * inv_sqrt
            own_scores = jnp.einsum('sgrd,mrd->sgrm', head_queries, own_keys) * inv_sqrt
            visible = allowed[:, None]
            run_max = jnp.maximum(lax.optimization_barrier(jnp.max(jnp.where(visible, scores, neg_fill), axis=-1)), lax.optimization_barrier(jnp.max(jnp.where(own_mask, own_scores, neg_fill), axis=-1)))
            weights = jnp.where(visible, jnp.exp(scores - run_max[..., None]), 0.0)
            own_weights = jnp.where(own_mask, jnp.exp(own_scores - run_max[..., None]), 0.0)
            run_sum = lax.optimization_barrier(jnp.sum(weights, axis=-1)) + lax.optimization_barrier(jnp.sum(own_weights, axis=-1))
            rounded = lax.optimization_barrier(weights.astype(jnp.bfloat16)).astype(jnp.float32)
            own_rounded = lax.optimization_barrier(own_weights.astype(jnp.bfloat16)).astype(jnp.float32)
            summed = jnp.einsum('sgrt,td->sgrd', rounded, head_values) + jnp.einsum('sgrm,mrd->sgrd', own_rounded, own_values)
            return (summed / run_sum[..., None]).astype(jnp.bfloat16)
        outputs = lax.map(one_head, (grouped, keys_all, values_all, step_rows))
        return jnp.moveaxis(outputs, 0, 1).reshape(STEPS, HEADS, row_span, HEAD_DIM)
    stacked = lax.map(one_block, jnp.arange(TOKENS // row_span, dtype=jnp.int32))
    attended = jnp.moveaxis(stacked, 0, 2).reshape(STEPS, HEADS, TOKENS, HEAD_DIM)
    return (attended, kv_cache)
```

```python
import functools
import math

import jax
import jax.numpy as jnp
from jax import lax
from jax.experimental import pallas as pl
from jax.experimental.pallas import tpu as pltpu
from jax.sharding import PartitionSpec as P

neg_fill = -1e30
MESH = pl.DeviceIdType.MESH
CORES = 2


def flipped(index, mask, count):
    result, bit = 0, 1
    while bit < count:
        own = (index // bit) % 2
        result = result + bit * ((1 - own) if mask & bit else own)
        bit *= 2
    return result


def kv_kernel(
    sections, shards, feature_width,
    feat_ref, gain_ref, weight_ref, kv_ref,
    weight_buf, scaled, own_part, send_buf, recv_buf, square_send, square_recv,
    weight_sem, rs_send, rs_recv, sq_send, sq_recv, chain_send, chain_recv, twin_send, twin_recv,
):
    section = lax.axis_index("section")
    shard = lax.axis_index("seq")
    groups, _, tokens, width = kv_ref.shape
    pairs = shards // CORES
    pair, core = shard // CORES, shard % CORES
    twin = pair * CORES + 1 - core
    later, earlier = shard + CORES, shard - CORES
    order = [(g, k) for g in range(groups) for k in range(sections - 1, -1, -1)]

    def weight_copy(slot):
        g, k = order[slot]
        column = pl.multiple_of((flipped(section, k, sections) * groups + g) * width, width)
        return pltpu.make_async_copy(
            weight_ref.at[:, pl.ds(column, width)], weight_buf.at[slot], weight_sem.at[slot]
        )

    for slot in range(len(order)):
        weight_copy(slot).start()

    barrier = pltpu.get_barrier_semaphore()
    for k in range(1, sections):
        pl.semaphore_signal(
            barrier, inc=1, device_id={"section": flipped(section, k, sections)}, device_id_type=MESH
        )
    pl.semaphore_signal(barrier, inc=1, device_id={"seq": twin}, device_id_type=MESH)

    @pl.when(pair < pairs - 1)
    def _():
        pl.semaphore_signal(barrier, inc=1, device_id={"seq": later}, device_id_type=MESH)

    @pl.when(pair > 0)
    def _():
        pl.semaphore_signal(barrier, inc=1, device_id={"seq": earlier}, device_id_type=MESH)

    floated = feat_ref[...].astype(jnp.float32)
    scaled[...] = (floated * gain_ref[...]).astype(jnp.bfloat16)
    squares = jnp.sum(floated * floated, axis=1, keepdims=True)
    square_rows = jnp.transpose(jnp.broadcast_to(squares, (tokens, tokens)))[:8]
    square_send[...] = square_rows

    pl.semaphore_wait(barrier, sections + jnp.where(pair > 0, 1, 0) + jnp.where(pair < pairs - 1, 1, 0))

    def square_copy(k):
        return pltpu.make_async_remote_copy(
            src_ref=square_send, dst_ref=square_recv.at[k - 1],
            send_sem=sq_send.at[k - 1], recv_sem=sq_recv.at[k - 1],
            device_id={"section": flipped(section, k, sections)}, device_id_type=MESH,
        )

    def part_copy(g, k):
        return pltpu.make_async_remote_copy(
            src_ref=send_buf.at[g, k - 1], dst_ref=recv_buf.at[g, k - 1],
            send_sem=rs_send.at[g, k - 1], recv_sem=rs_recv.at[g, k - 1],
            device_id={"section": flipped(section, k, sections)}, device_id_type=MESH,
        )

    def chain_copy(g, hop):
        place = kv_ref.at[g, shard - CORES * hop]
        return pltpu.make_async_remote_copy(
            src_ref=place, dst_ref=place,
            send_sem=chain_send.at[g, hop], recv_sem=chain_recv.at[g, hop],
            device_id={"seq": later}, device_id_type=MESH,
        )

    def twin_copy(g, hop):
        place = kv_ref.at[g, shard - CORES * hop]
        return pltpu.make_async_remote_copy(
            src_ref=place, dst_ref=place,
            send_sem=twin_send.at[g, hop], recv_sem=twin_recv.at[g, hop],
            device_id={"seq": twin}, device_id_type=MESH,
        )

    def chain_arrival(g, hop):
        place = kv_ref.at[g, shard - CORES * hop]
        return pltpu.make_async_remote_copy(
            src_ref=place, dst_ref=place,
            send_sem=chain_send.at[g, hop - 1], recv_sem=chain_recv.at[g, hop - 1],
            device_id={"seq": later}, device_id_type=MESH,
        )

    def twin_arrival(g, hop):
        place = kv_ref.at[g, twin - CORES * hop]
        return pltpu.make_async_remote_copy(
            src_ref=place, dst_ref=place,
            send_sem=twin_send.at[g, hop], recv_sem=twin_recv.at[g, hop],
            device_id={"seq": twin}, device_id_type=MESH,
        )

    for k in range(1, sections):
        square_copy(k).start()

    for slot, (g, k) in enumerate(order):
        weight_copy(slot).wait()
        part = jnp.dot(scaled[...], weight_buf[slot], preferred_element_type=jnp.float32)
        if k:
            send_buf[g, k - 1] = part.astype(jnp.bfloat16)
            part_copy(g, k).start()
        else:
            own_part[g] = part

    total = square_rows
    for k in range(1, sections):
        square_copy(k).wait()
        total = total + square_recv[k - 1]
    mean = jnp.transpose(jnp.broadcast_to(total[:1], (tokens, tokens))) / feature_width
    inverse = jnp.concatenate([lax.rsqrt(mean + 1e-05)] * (width // tokens), axis=1)

    for g in range(groups):
        summed = own_part[g]
        for k in range(sections - 1, 0, -1):
            part_copy(g, k).wait_recv()
            summed = summed + recv_buf[g, k - 1].astype(jnp.float32)
        kv_ref[g, shard] = (summed * inverse).astype(jnp.bfloat16)

        @pl.when(pair < pairs - 1)
        def _():
            chain_copy(g, 0).start()

        twin_copy(g, 0).start()

    for hop in range(1, pairs):
        @pl.when(hop <= pair)
        def _():
            for g in range(groups):
                chain_arrival(g, hop).wait_recv()

                @pl.when(pair < pairs - 1)
                def _():
                    chain_copy(g, hop).start()

                twin_copy(g, hop).start()

    for hop in range(pairs):
        @pl.when(hop <= pair)
        def _():
            for g in range(groups):
                twin_arrival(g, hop).wait_recv()
                twin_copy(g, hop).wait_send()

                @pl.when(pair < pairs - 1)
                def _():
                    chain_copy(g, hop).wait_send()

    for g in range(groups):
        for k in range(1, sections):
            part_copy(g, k).wait_send()


def attend_kernel(
    block_len, entries,
    doc_smem, list_smem, docs_ref, query_ref, step_ref, kv_ref, out_ref, cache_ref,
    bias, step_scores, scores, top, total, acc,
):
    shard = lax.axis_index("seq")
    step = pl.program_id(1)
    _, heads, tokens, head_dim = query_ref.shape
    steps = step_ref.shape[0]
    shards = kv_ref.shape[1]
    chunk = CORES * tokens
    chunks = shards // CORES
    pair = shard // CORES
    scale = math.log2(math.e) / math.sqrt(head_dim)
    contract_last = (((1,), (1,)), ((), ()))

    cache_ref[0] = kv_ref[0, shard]

    first_doc = doc_smem[shard * tokens]
    lowest = jnp.int32(0)
    for c in range(chunks):
        lowest = lowest + jnp.where(doc_smem[c * chunk + chunk - 1] < first_doc, 1, 0)

    row = lax.broadcasted_iota(jnp.int32, (tokens, tokens), 0)
    column = lax.broadcasted_iota(jnp.int32, (tokens, tokens), 1)
    lane = lax.broadcasted_iota(jnp.int32, (1, tokens), 1)
    diagonal = jnp.where(row == column, 0.0, neg_fill)
    own_docs = docs_ref[pl.ds(shard, 1), :].astype(jnp.float32)
    row_docs = jnp.transpose(jnp.broadcast_to(own_docs, (tokens, tokens)))
    row_blocks = tokens // block_len

    def score(queries, keys):
        return lax.dot_general(queries, keys, contract_last, preferred_element_type=jnp.float32)

    for h in range(heads):
        first = score(query_ref[0, h], step_ref[0, 0, :, :head_dim]) + diagonal
        step_scores[0, h] = first
        top[h] = first
    for m in range(1, steps):
        @pl.when(m <= step)
        def _():
            for h in range(heads):
                more = score(query_ref[0, h], step_ref[m, 0, :, :head_dim]) + diagonal
                step_scores[m, h] = more
                top[h] = jnp.maximum(top[h], more)

    def first_pass(c, _):
        halves = []
        for half in range(CORES):
            key_shard = c * CORES + half
            key_block = key_shard * row_blocks + lane // block_len
            listed = []
            for r in range(row_blocks):
                marks = jnp.full((1, tokens), neg_fill, jnp.float32)
                for e in range(entries):
                    entry = list_smem[(step * shards + shard) * row_blocks * entries + r * entries + e]
                    marks = jnp.where(key_block == entry, 0.0, marks)
                listed.append(marks)
            marks = jnp.broadcast_to(listed[-1], (tokens, tokens))
            for r in range(row_blocks - 2, -1, -1):
                marks = jnp.where(row < (r + 1) * block_len, listed[r], marks)
            key_docs = docs_ref[pl.ds(key_shard, 1), :].astype(jnp.float32)
            marks = jnp.where(row_docs == key_docs, marks, neg_fill)
            marks = jnp.where(key_shard * tokens + column <= shard * tokens + row, marks, neg_fill)
            halves.append(marks)
        bias[...] = jnp.concatenate(halves, axis=1)
        keys = kv_ref[0, pl.ds(c * CORES, CORES), :, :head_dim].reshape(chunk, head_dim)
        for h in range(heads):
            found = score(query_ref[0, h], keys) + bias[...]
            scores[c, h] = found
            top[h] = jnp.maximum(top[h], jnp.maximum(found[:, :tokens], found[:, tokens:]))
        return 0

    lax.fori_loop(lowest, pair + 1, first_pass, 0)

    for h in range(heads):
        highest = jnp.max(top[h], axis=1, keepdims=True) * scale
        top[h] = jnp.broadcast_to(highest, (tokens, tokens))

    for h in range(heads):
        weight = jnp.exp2(step_scores[0, h] * scale - top[h])
        total[h] = weight
        acc[h] = jnp.dot(
            weight.astype(jnp.bfloat16), step_ref[0, 0, :, head_dim:], preferred_element_type=jnp.float32
        )
    for m in range(1, steps):
        @pl.when(m <= step)
        def _():
            for h in range(heads):
                weight = jnp.exp2(step_scores[m, h] * scale - top[h])
                total[h] += weight
                acc[h] += jnp.dot(
                    weight.astype(jnp.bfloat16), step_ref[m, 0, :, head_dim:],
                    preferred_element_type=jnp.float32,
                )

    def second_pass(c, _):
        values = kv_ref[0, pl.ds(c * CORES, CORES), :, head_dim:].reshape(chunk, head_dim)
        for h in range(heads):
            highest = jnp.concatenate([top[h]] * CORES, axis=1)
            weight = jnp.exp2(scores[c, h] * scale - highest)
            total[h] += weight[:, :tokens] + weight[:, tokens:]
            acc[h] += jnp.dot(weight.astype(jnp.bfloat16), values, preferred_element_type=jnp.float32)
        return 0

    lax.fori_loop(lowest, pair + 1, second_pass, 0)

    for h in range(heads):
        denominator = jnp.sum(total[h], axis=1, keepdims=True)
        out_ref[0, h] = (acc[h] / denominator).astype(out_ref.dtype)


def per_device(sections, shards, features, norm_gain, kv_weight, queries, step_kv, doc_ids, block_lists):
    steps, local_heads, tokens, head_dim = queries.shape
    groups = step_kv.shape[1]
    group_size = local_heads // groups
    width = 2 * head_dim
    local_width = features.shape[1]
    blocks, entries = block_lists.shape[1:]
    block_len = doc_ids.shape[0] // blocks
    pairs = shards // CORES
    others = sections - 1
    dma = pltpu.SemaphoreType.DMA
    vmem = pl.BlockSpec(memory_space=pltpu.VMEM)

    kv_all = pl.pallas_call(
        functools.partial(kv_kernel, sections, shards, local_width * sections),
        out_shape=jax.ShapeDtypeStruct((groups, shards, tokens, width), jnp.bfloat16),
        in_specs=[vmem, vmem, pl.BlockSpec(memory_space=pl.ANY)],
        out_specs=vmem,
        scratch_shapes=[
            pltpu.VMEM((groups * sections, local_width, width), jnp.bfloat16),
            pltpu.VMEM((tokens, local_width), jnp.bfloat16),
            pltpu.VMEM((groups, tokens, width), jnp.float32),
            pltpu.VMEM((groups, others, tokens, width), jnp.bfloat16),
            pltpu.VMEM((groups, others, tokens, width), jnp.bfloat16),
            pltpu.VMEM((8, tokens), jnp.float32),
            pltpu.VMEM((others, 8, tokens), jnp.float32),
            dma((groups * sections,)),
            dma((groups, others)),
            dma((groups, others)),
            dma((others,)),
            dma((others,)),
            dma((groups, pairs)),
            dma((groups, pairs)),
            dma((groups, pairs)),
            dma((groups, pairs)),
        ],
        compiler_params=pltpu.CompilerParams(
            collective_id=0, has_side_effects=True, vmem_limit_bytes=32 * 1024 * 1024
        ),
    )(features, norm_gain.reshape(1, local_width), kv_weight)

    smem = pl.BlockSpec(memory_space=pltpu.SMEM)
    square = pltpu.VMEM((group_size, tokens, tokens), jnp.float32)
    attended, kv_cache = pl.pallas_call(
        functools.partial(attend_kernel, block_len, entries),
        grid=(groups, steps),
        out_shape=(
            jax.ShapeDtypeStruct(queries.shape, jnp.bfloat16),
            jax.ShapeDtypeStruct((groups, tokens, width), jnp.bfloat16),
        ),
        in_specs=[
            smem,
            smem,
            vmem,
            pl.BlockSpec((1, group_size, tokens, head_dim), lambda g, s: (s, g, 0, 0)),
            pl.BlockSpec((steps, 1, tokens, width), lambda g, s: (0, g, 0, 0)),
            pl.BlockSpec((1, shards, tokens, width), lambda g, s: (g, 0, 0, 0)),
        ],
        out_specs=(
            pl.BlockSpec((1, group_size, tokens, head_dim), lambda g, s: (s, g, 0, 0)),
            pl.BlockSpec((1, tokens, width), lambda g, s: (g, 0, 0)),
        ),
        scratch_shapes=[
            pltpu.VMEM((tokens, CORES * tokens), jnp.float32),
            pltpu.VMEM((steps, group_size, tokens, tokens), jnp.float32),
            pltpu.VMEM((pairs, group_size, tokens, CORES * tokens), jnp.float32),
            square,
            square,
            pltpu.VMEM((group_size, tokens, head_dim), jnp.float32),
        ],
        compiler_params=pltpu.CompilerParams(vmem_limit_bytes=48 * 1024 * 1024),
    )(
        doc_ids,
        block_lists.reshape(-1),
        doc_ids.reshape(shards, tokens),
        queries,
        step_kv,
        kv_all,
    )
    return (attended, kv_cache)


def solution(mesh):
    in_specs = (
        P("seq", "section"),
        P("section"),
        P("section", None),
        P(None, "section", "seq", None),
        P(None, "section", "seq", None),
        P(),
        P(),
    )
    out_specs = (P(None, "section", "seq", None), P("section", "seq", None))
    body = functools.partial(per_device, mesh.shape["section"], mesh.shape["seq"])
    return jax.shard_map(body, mesh=mesh, in_specs=in_specs, out_specs=out_specs, check_vma=False)
```

```python
import functools
import math

import jax
import jax.numpy as jnp
from jax import lax
from jax.experimental import pallas as pl
from jax.experimental.pallas import tpu as pltpu
from jax.sharding import PartitionSpec as P

neg_fill = -1e30
MESH = pl.DeviceIdType.MESH
CORES = 2


def flipped(index, mask, count):
    result, bit = 0, 1
    while bit < count:
        own = (index // bit) % 2
        result = result + bit * ((1 - own) if mask & bit else own)
        bit *= 2
    return result


def kv_kernel(
    sections, shards, feature_width,
    feat_ref, gain_ref, weight_ref, kv_ref,
    features, gain, weight_buf, scaled, own_part, send_buf, recv_buf, square_send, square_recv,
    load_sem, weight_sem, rs_send, rs_recv, sq_send, sq_recv, chain_send, chain_recv, twin_send, twin_recv,
):
    section = lax.axis_index("section")
    shard = lax.axis_index("seq")
    groups, _, tokens, width = kv_ref.shape
    pairs = shards // CORES
    pair, core = shard // CORES, shard % CORES
    twin = pair * CORES + 1 - core
    later, earlier = shard + CORES, shard - CORES
    order = [(g, k) for g in range(groups) for k in range(sections - 1, -1, -1)]

    def weight_copy(slot):
        g, k = order[slot]
        column = pl.multiple_of((flipped(section, k, sections) * groups + g) * width, width)
        return pltpu.make_async_copy(
            weight_ref.at[:, pl.ds(column, width)], weight_buf.at[slot], weight_sem.at[slot]
        )

    feature_load = pltpu.make_async_copy(feat_ref, features, load_sem.at[0])
    gain_load = pltpu.make_async_copy(gain_ref, gain, load_sem.at[1])
    feature_load.start()
    gain_load.start()
    for slot in range(len(order)):
        weight_copy(slot).start()

    barrier = pltpu.get_barrier_semaphore()
    for k in range(1, sections):
        pl.semaphore_signal(
            barrier, inc=1, device_id={"section": flipped(section, k, sections)}, device_id_type=MESH
        )
    pl.semaphore_signal(barrier, inc=1, device_id={"seq": twin}, device_id_type=MESH)

    @pl.when(pair < pairs - 1)
    def _():
        pl.semaphore_signal(barrier, inc=1, device_id={"seq": later}, device_id_type=MESH)

    @pl.when(pair > 0)
    def _():
        pl.semaphore_signal(barrier, inc=1, device_id={"seq": earlier}, device_id_type=MESH)

    feature_load.wait()
    gain_load.wait()
    floated = features[...].astype(jnp.float32)
    squares = jnp.sum(floated * floated, axis=1, keepdims=True)
    square_rows = jnp.transpose(jnp.broadcast_to(squares, (tokens, tokens)))[:8]
    square_send[...] = square_rows

    pl.semaphore_wait(barrier, sections + jnp.where(pair > 0, 1, 0) + jnp.where(pair < pairs - 1, 1, 0))

    def square_copy(k):
        return pltpu.make_async_remote_copy(
            src_ref=square_send, dst_ref=square_recv.at[k - 1],
            send_sem=sq_send.at[k - 1], recv_sem=sq_recv.at[k - 1],
            device_id={"section": flipped(section, k, sections)}, device_id_type=MESH,
        )

    def part_copy(g, k):
        return pltpu.make_async_remote_copy(
            src_ref=send_buf.at[g, k - 1], dst_ref=recv_buf.at[g, k - 1],
            send_sem=rs_send.at[g, k - 1], recv_sem=rs_recv.at[g, k - 1],
            device_id={"section": flipped(section, k, sections)}, device_id_type=MESH,
        )

    def chain_copy(g, hop):
        place = kv_ref.at[g, shard - CORES * hop]
        return pltpu.make_async_remote_copy(
            src_ref=place, dst_ref=place,
            send_sem=chain_send.at[g, hop], recv_sem=chain_recv.at[g, hop],
            device_id={"seq": later}, device_id_type=MESH,
        )

    def twin_copy(g, hop):
        place = kv_ref.at[g, shard - CORES * hop]
        return pltpu.make_async_remote_copy(
            src_ref=place, dst_ref=place,
            send_sem=twin_send.at[g, hop], recv_sem=twin_recv.at[g, hop],
            device_id={"seq": twin}, device_id_type=MESH,
        )

    def chain_arrival(g, hop):
        place = kv_ref.at[g, shard - CORES * hop]
        return pltpu.make_async_remote_copy(
            src_ref=place, dst_ref=place,
            send_sem=chain_send.at[g, hop - 1], recv_sem=chain_recv.at[g, hop - 1],
            device_id={"seq": later}, device_id_type=MESH,
        )

    def twin_arrival(g, hop):
        place = kv_ref.at[g, twin - CORES * hop]
        return pltpu.make_async_remote_copy(
            src_ref=place, dst_ref=place,
            send_sem=twin_send.at[g, hop], recv_sem=twin_recv.at[g, hop],
            device_id={"seq": twin}, device_id_type=MESH,
        )

    for k in range(1, sections):
        square_copy(k).start()
    total = square_rows
    for k in range(1, sections):
        square_copy(k).wait()
        total = total + square_recv[k - 1]
    mean = jnp.transpose(jnp.broadcast_to(total[:1], (tokens, tokens))) / feature_width
    inverse = lax.rsqrt(mean + 1e-05)
    for first in range(0, features.shape[1], tokens):
        part = pl.ds(first, tokens)
        scaled[:, part] = (
            features[:, part].astype(jnp.float32) * inverse * gain[:, part]
        ).astype(jnp.bfloat16)

    for slot, (g, k) in enumerate(order):
        weight_copy(slot).wait()
        part = jnp.dot(scaled[...], weight_buf[slot], preferred_element_type=jnp.float32)
        if k:
            send_buf[g, k - 1] = part.astype(jnp.bfloat16)
            part_copy(g, k).start()
        else:
            own_part[g] = part

    for g in range(groups):
        summed = own_part[g]
        for k in range(sections - 1, 0, -1):
            part_copy(g, k).wait_recv()
            summed = summed + recv_buf[g, k - 1].astype(jnp.float32)
        kv_ref[g, shard] = summed.astype(jnp.bfloat16)

        @pl.when(pair < pairs - 1)
        def _():
            chain_copy(g, 0).start()

        twin_copy(g, 0).start()

    for hop in range(1, pairs):
        @pl.when(hop <= pair)
        def _():
            for g in range(groups):
                chain_arrival(g, hop).wait_recv()

                @pl.when(pair < pairs - 1)
                def _():
                    chain_copy(g, hop).start()

                twin_copy(g, hop).start()

    for hop in range(pairs):
        @pl.when(hop <= pair)
        def _():
            for g in range(groups):
                twin_arrival(g, hop).wait_recv()
                twin_copy(g, hop).wait_send()

                @pl.when(pair < pairs - 1)
                def _():
                    chain_copy(g, hop).wait_send()

    for g in range(groups):
        for k in range(1, sections):
            part_copy(g, k).wait_send()


def attend_kernel(
    block_len,
    doc_smem, list_smem, docs_ref, query_ref, step_ref, kv_ref, out_ref, cache_ref,
    bias, step_scores, scores, top, acc,
):
    shard = lax.axis_index("seq")
    step, group = pl.program_id(0), pl.program_id(1)
    _, heads, tokens, head_dim = query_ref.shape
    steps = step_ref.shape[0]
    groups, shards = kv_ref.shape[:2]
    entries = list_smem.shape[2]
    chunk = CORES * tokens
    chunks = shards // CORES
    pair = shard // CORES
    scale = math.log2(math.e) / math.sqrt(head_dim)
    contract_last = (((1,), (1,)), ((), ()))
    rows = [slice(h * tokens, (h + 1) * tokens) for h in range(heads)]

    first_doc = doc_smem[shard * tokens]
    lowest = jnp.int32(0)
    for c in range(chunks):
        lowest = lowest + jnp.where(doc_smem[c * chunk + chunk - 1] < first_doc, 1, 0)

    row = lax.broadcasted_iota(jnp.int32, (tokens, tokens), 0)
    column = lax.broadcasted_iota(jnp.int32, (tokens, tokens), 1)
    row_blocks = tokens // block_len

    @pl.when(group == 0)
    def _():
        for g in range(groups):
            cache_ref[g] = kv_ref[g, shard]
        lane = lax.broadcasted_iota(jnp.int32, (1, tokens), 1)
        own_docs = docs_ref[pl.ds(shard, 1), :].astype(jnp.float32)
        row_docs = jnp.transpose(jnp.broadcast_to(own_docs, (tokens, tokens)))

        def fill(c, _):
            for half in range(CORES):
                key_shard = c * CORES + half
                key_block = key_shard * row_blocks + lane // block_len
                listed = []
                for r in range(row_blocks):
                    marks = jnp.full((1, tokens), neg_fill, jnp.float32)
                    for e in range(entries):
                        entry = list_smem[step, shard * row_blocks + r, e]
                        marks = jnp.where(key_block == entry, 0.0, marks)
                    listed.append(marks)
                marks = jnp.broadcast_to(listed[-1], (tokens, tokens))
                for r in range(row_blocks - 2, -1, -1):
                    marks = jnp.where(row < (r + 1) * block_len, listed[r], marks)
                key_docs = docs_ref[pl.ds(key_shard, 1), :].astype(jnp.float32)
                marks = jnp.where(row_docs == key_docs, marks, neg_fill)
                marks = jnp.where(key_shard * tokens + column <= shard * tokens + row, marks, neg_fill)
                bias[c, :, half * tokens:(half + 1) * tokens] = marks
            return 0

        lax.fori_loop(lowest, pair + 1, fill, 0)

    queries = query_ref[0].reshape(heads * tokens, head_dim)
    diagonal = jnp.where(row == column, 0.0, neg_fill)

    def score(keys):
        return lax.dot_general(queries, keys, contract_last, preferred_element_type=jnp.float32)

    def extended(values):
        return jnp.concatenate([values, jnp.ones_like(values)], axis=1)

    def step_first(m):
        found = score(step_ref[m, group, :, :head_dim])
        for r in rows:
            masked = found[r] + diagonal
            step_scores[m, r, :] = masked
            top[r, :] = jnp.maximum(top[r, :], masked) if m else masked

    def step_second(m):
        weights = [
            jnp.exp2(step_scores[m, r, :] * scale - top[r, :]).astype(jnp.bfloat16) for r in rows
        ]
        return jnp.dot(
            jnp.concatenate(weights, axis=0), extended(step_ref[m, group, :, head_dim:]),
            preferred_element_type=jnp.float32,
        )

    def first_pass(c, many):
        keys = kv_ref[group, pl.ds(c * CORES, many * CORES), :, :head_dim].reshape(many * chunk, head_dim)
        found = score(keys)
        for r in rows:
            highest = top[r, :]
            for i in range(many):
                masked = found[r, i * chunk:(i + 1) * chunk] + bias[c + i]
                scores[c + i, r, :] = masked
                highest = jnp.maximum(highest, jnp.maximum(masked[:, :tokens], masked[:, tokens:]))
            top[r, :] = highest

    def second_pass(c, many):
        values = kv_ref[group, pl.ds(c * CORES, many * CORES), :, head_dim:].reshape(many * chunk, head_dim)
        weights = []
        for r in rows:
            highest = jnp.concatenate([top[r, :]] * CORES, axis=1)
            weights.append(jnp.concatenate(
                [jnp.exp2(scores[c + i, r, :] * scale - highest).astype(jnp.bfloat16) for i in range(many)],
                axis=1,
            ))
        acc[...] += jnp.dot(
            jnp.concatenate(weights, axis=0), extended(values), preferred_element_type=jnp.float32
        )

    def over_chunks(run):
        count = pair + 1 - lowest

        def body(i, _):
            run(lowest + 2 * i, 2)
            return 0

        lax.fori_loop(0, count // 2, body, 0)

        @pl.when(count % 2 == 1)
        def _():
            run(pair, 1)

    step_first(0)
    for m in range(1, steps):
        pl.when(m <= step)(functools.partial(step_first, m))
    over_chunks(first_pass)

    for r in rows:
        highest = jnp.max(top[r, :], axis=1, keepdims=True) * scale
        top[r, :] = jnp.broadcast_to(highest, (tokens, tokens))

    acc[...] = step_second(0)
    for m in range(1, steps):
        @pl.when(m <= step)
        def _():
            acc[...] += step_second(m)
    over_chunks(second_pass)

    for h, r in enumerate(rows):
        out_ref[0, h] = (acc[r, :head_dim] / acc[r, head_dim:]).astype(out_ref.dtype)


def per_device(sections, shards, features, norm_gain, kv_weight, queries, step_kv, doc_ids, block_lists):
    steps, local_heads, tokens, head_dim = queries.shape
    groups = step_kv.shape[1]
    group_size = local_heads // groups
    width = 2 * head_dim
    local_width = features.shape[1]
    blocks = block_lists.shape[1]
    block_len = doc_ids.shape[0] // blocks
    pairs = shards // CORES
    others = sections - 1
    dma = pltpu.SemaphoreType.DMA
    vmem = pl.BlockSpec(memory_space=pltpu.VMEM)

    kv_all = pl.pallas_call(
        functools.partial(kv_kernel, sections, shards, local_width * sections),
        out_shape=jax.ShapeDtypeStruct((groups, shards, tokens, width), jnp.bfloat16),
        in_specs=[pl.BlockSpec(memory_space=pl.ANY)] * 3,
        out_specs=vmem,
        scratch_shapes=[
            pltpu.VMEM((tokens, local_width), jnp.bfloat16),
            pltpu.VMEM((1, local_width), jnp.float32),
            pltpu.VMEM((groups * sections, local_width, width), jnp.bfloat16),
            pltpu.VMEM((tokens, local_width), jnp.bfloat16),
            pltpu.VMEM((groups, tokens, width), jnp.float32),
            pltpu.VMEM((groups, others, tokens, width), jnp.bfloat16),
            pltpu.VMEM((groups, others, tokens, width), jnp.bfloat16),
            pltpu.VMEM((8, tokens), jnp.float32),
            pltpu.VMEM((others, 8, tokens), jnp.float32),
            dma((2,)),
            dma((groups * sections,)),
            dma((groups, others)),
            dma((groups, others)),
            dma((others,)),
            dma((others,)),
            dma((groups, pairs)),
            dma((groups, pairs)),
            dma((groups, pairs)),
            dma((groups, pairs)),
        ],
        compiler_params=pltpu.CompilerParams(
            collective_id=0, has_side_effects=True, vmem_limit_bytes=60 * 1024 * 1024
        ),
    )(features, norm_gain.reshape(1, local_width), kv_weight)

    smem = pl.BlockSpec(memory_space=pltpu.SMEM)
    attended, kv_cache = pl.pallas_call(
        functools.partial(attend_kernel, block_len),
        grid=(steps, groups),
        out_shape=(
            jax.ShapeDtypeStruct(queries.shape, jnp.bfloat16),
            jax.ShapeDtypeStruct((groups, tokens, width), jnp.bfloat16),
        ),
        in_specs=[
            smem,
            smem,
            vmem,
            pl.BlockSpec((1, group_size, tokens, head_dim), lambda s, g: (s, g, 0, 0)),
            vmem,
            vmem,
        ],
        out_specs=(
            pl.BlockSpec((1, group_size, tokens, head_dim), lambda s, g: (s, g, 0, 0)),
            vmem,
        ),
        scratch_shapes=[
            pltpu.VMEM((pairs, tokens, CORES * tokens), jnp.float32),
            pltpu.VMEM((steps, group_size * tokens, tokens), jnp.float32),
            pltpu.VMEM((pairs, group_size * tokens, CORES * tokens), jnp.float32),
            pltpu.VMEM((group_size * tokens, tokens), jnp.float32),
            pltpu.VMEM((group_size * tokens, width), jnp.float32),
        ],
        compiler_params=pltpu.CompilerParams(vmem_limit_bytes=48 * 1024 * 1024),
    )(
        doc_ids,
        block_lists,
        doc_ids.reshape(shards, tokens),
        queries,
        step_kv,
        kv_all,
    )
    return (attended, kv_cache)


def solution(mesh):
    in_specs = (
        P("seq", "section"),
        P("section"),
        P("section", None),
        P(None, "section", "seq", None),
        P(None, "section", "seq", None),
        P(),
        P(),
    )
    out_specs = (P(None, "section", "seq", None), P("section", "seq", None))
    body = functools.partial(per_device, mesh.shape["section"], mesh.shape["seq"])
    return jax.shard_map(body, mesh=mesh, in_specs=in_specs, out_specs=out_specs, check_vma=False)
```

```python
import functools
import math

import jax
import jax.numpy as jnp
from jax import lax
from jax.experimental import pallas as pl
from jax.experimental.pallas import tpu as pltpu
from jax.sharding import PartitionSpec as P

neg_fill = -1e30
MESH = pl.DeviceIdType.MESH
CORES = 2


def flipped(index, mask, count):
    result, bit = 0, 1
    while bit < count:
        own = (index // bit) % 2
        result = result + bit * ((1 - own) if mask & bit else own)
        bit *= 2
    return result


def fused_kernel(
    sections, shards, feature_width, block_len,
    feat_ref, gain_ref, weight_ref, query_ref, step_ref, docs_ref, list_smem,
    out_ref, cache_ref,
    features, gain, queries, step_kv, weight_buf, scaled, own_part, send_buf, recv_buf,
    square_send, square_recv, kv, bias, top, acc,
    load_sem, weight_sem, rs_send, rs_recv, sq_send, sq_recv,
    direct_send, direct_recv, twin_send, twin_recv,
):
    section = lax.axis_index("section")
    shard = lax.axis_index("seq")
    groups, _, tokens, width = kv.shape
    steps, local_heads, _, head_dim = queries.shape
    heads = local_heads // groups
    entries = list_smem.shape[2]
    chunk = CORES * tokens
    pairs = shards // CORES
    pair, core = shard // CORES, shard % CORES
    twin = pair * CORES + 1 - core
    scale = math.log2(math.e) / math.sqrt(head_dim)
    order = [(g, k) for g in range(groups) for k in range(sections - 1, -1, -1)]
    row_blocks = tokens // block_len

    def weight_copy(slot):
        g, k = order[slot]
        column = pl.multiple_of((flipped(section, k, sections) * groups + g) * width, width)
        return pltpu.make_async_copy(
            weight_ref.at[:, pl.ds(column, width)], weight_buf.at[slot], weight_sem.at[slot]
        )

    feature_load = pltpu.make_async_copy(feat_ref, features, load_sem.at[0])
    gain_load = pltpu.make_async_copy(gain_ref, gain, load_sem.at[1])
    step_load = pltpu.make_async_copy(step_ref, step_kv, load_sem.at[2])
    query_load = pltpu.make_async_copy(query_ref, queries, load_sem.at[3])
    for load in (feature_load, gain_load, step_load, query_load):
        load.start()
    for slot in range(len(order)):
        weight_copy(slot).start()

    barrier = pltpu.get_barrier_semaphore()
    for k in range(1, sections):
        pl.semaphore_signal(
            barrier, inc=1, device_id={"section": flipped(section, k, sections)}, device_id_type=MESH
        )
    pl.semaphore_signal(barrier, inc=1, device_id={"seq": twin}, device_id_type=MESH)
    for d in range(1, pairs):
        other = (pair + d) % pairs * CORES + core
        pl.semaphore_signal(barrier, inc=1, device_id={"seq": other}, device_id_type=MESH)

    feature_load.wait()
    gain_load.wait()
    floated = features[...].astype(jnp.float32)
    squares = jnp.sum(floated * floated, axis=1, keepdims=True)
    square_rows = jnp.transpose(jnp.broadcast_to(squares, (tokens, tokens)))[:8]
    square_send[...] = square_rows

    pl.semaphore_wait(barrier, sections + pairs - 1)

    def square_copy(k):
        return pltpu.make_async_remote_copy(
            src_ref=square_send, dst_ref=square_recv.at[k - 1],
            send_sem=sq_send.at[k - 1], recv_sem=sq_recv.at[k - 1],
            device_id={"section": flipped(section, k, sections)}, device_id_type=MESH,
        )

    def part_copy(g, k):
        return pltpu.make_async_remote_copy(
            src_ref=send_buf.at[g, k - 1], dst_ref=recv_buf.at[g, k - 1],
            send_sem=rs_send.at[g, k - 1], recv_sem=rs_recv.at[g, k - 1],
            device_id={"section": flipped(section, k, sections)}, device_id_type=MESH,
        )

    def direct_copy(g, d):
        place = kv.at[g, shard]
        return pltpu.make_async_remote_copy(
            src_ref=place, dst_ref=place,
            send_sem=direct_send.at[g, d], recv_sem=direct_recv.at[g, d],
            device_id={"seq": shard + CORES * d}, device_id_type=MESH,
        )

    def direct_arrival(g, d):
        place = kv.at[g, shard - CORES * d]
        return pltpu.make_async_remote_copy(
            src_ref=place, dst_ref=place,
            send_sem=direct_send.at[g, d], recv_sem=direct_recv.at[g, d],
            device_id={"seq": twin}, device_id_type=MESH,
        )

    def twin_copy(g, hop):
        place = kv.at[g, shard - CORES * hop]
        return pltpu.make_async_remote_copy(
            src_ref=place, dst_ref=place,
            send_sem=twin_send.at[g, hop], recv_sem=twin_recv.at[g, hop],
            device_id={"seq": twin}, device_id_type=MESH,
        )

    def twin_arrival(g, hop):
        place = kv.at[g, twin - CORES * hop]
        return pltpu.make_async_remote_copy(
            src_ref=place, dst_ref=place,
            send_sem=twin_send.at[g, hop], recv_sem=twin_recv.at[g, hop],
            device_id={"seq": twin}, device_id_type=MESH,
        )

    def own_steps(h, _):
        g = h // heads
        part = pl.ds(pl.multiple_of(h % heads * tokens, tokens), tokens)
        keys = [step_kv[m, g, :, :head_dim].astype(jnp.float32) for m in range(steps)]
        values = [step_kv[m, g, :, head_dim:].astype(jnp.float32) for m in range(steps)]
        for s in range(steps):
            query = queries[s, h].astype(jnp.float32)
            found = [jnp.sum(query * keys[m], axis=1, keepdims=True) * scale for m in range(s + 1)]
            highest = functools.reduce(jnp.maximum, found)
            weights = [jnp.exp2(one - highest) for one in found]
            rounded = [w.astype(jnp.bfloat16).astype(jnp.float32) for w in weights]
            top[s, g, part, :] = jnp.broadcast_to(highest, (tokens, tokens))
            acc[s, g, part, :head_dim] = sum(w * values[m] for m, w in enumerate(rounded))
            acc[s, g, part, head_dim:] = jnp.broadcast_to(sum(weights), (tokens, head_dim))
        return 0

    def fill_bias(c, _):
        row = lax.broadcasted_iota(jnp.int32, (tokens, tokens), 0)
        column = lax.broadcasted_iota(jnp.int32, (tokens, tokens), 1)
        lane = lax.broadcasted_iota(jnp.int32, (1, tokens), 1)
        own_docs = docs_ref[pl.ds(shard, 1), :].astype(jnp.float32)
        row_docs = jnp.transpose(jnp.broadcast_to(own_docs, (tokens, tokens)))
        for half in range(CORES):
            key_shard = c * CORES + half
            key_block = key_shard * row_blocks + lane // block_len
            key_docs = docs_ref[pl.ds(key_shard, 1), :].astype(jnp.float32)
            shared = (row_docs == key_docs) & (key_shard * tokens + column <= shard * tokens + row)
            for s in range(steps):
                listed = []
                for r in range(row_blocks):
                    marks = jnp.full((1, tokens), neg_fill, jnp.float32)
                    for e in range(entries):
                        entry = list_smem[s, shard * row_blocks + r, e]
                        marks = jnp.where(key_block == entry, 0.0, marks)
                    listed.append(marks)
                marks = jnp.broadcast_to(listed[-1], (tokens, tokens))
                for r in range(row_blocks - 2, -1, -1):
                    marks = jnp.where(row < (r + 1) * block_len, listed[r], marks)
                bias[s, c, :, half * tokens:(half + 1) * tokens] = jnp.where(shared, marks, neg_fill)
        return 0

    for k in range(1, sections):
        square_copy(k).start()

    step_load.wait()
    query_load.wait()
    lax.fori_loop(0, local_heads // 2, own_steps, 0)

    total = square_rows
    for k in range(1, sections):
        square_copy(k).wait()
        total = total + square_recv[k - 1]
    mean = jnp.transpose(jnp.broadcast_to(total[:1], (tokens, tokens))) / feature_width
    inverse = lax.rsqrt(mean + 1e-05)
    for first in range(0, features.shape[1], tokens):
        part = pl.ds(first, tokens)
        scaled[:, part] = (
            features[:, part].astype(jnp.float32) * inverse * gain[:, part]
        ).astype(jnp.bfloat16)

    for slot, (g, k) in enumerate(order):
        weight_copy(slot).wait()
        part = jnp.dot(scaled[...], weight_buf[slot], preferred_element_type=jnp.float32)
        if k:
            send_buf[g, k - 1] = part.astype(jnp.bfloat16)
            part_copy(g, k).start()
        else:
            own_part[g] = part

    lax.fori_loop(local_heads // 2, local_heads, own_steps, 0)
    lax.fori_loop(0, pair + 1, fill_bias, 0)

    for g in range(groups):
        summed = own_part[g]
        for k in range(sections - 1, 0, -1):
            part_copy(g, k).wait_recv()
            summed = summed + recv_buf[g, k - 1].astype(jnp.float32)
        rounded = summed.astype(jnp.bfloat16)
        kv[g, shard] = rounded
        cache_ref[g] = rounded
        twin_copy(g, 0).start()

        def send(d, _):
            direct_copy(g, d).start()
            return 0

        lax.fori_loop(1, pairs - pair, send, 0)

    def attend(s, g, c):
        keys = kv[g, pl.ds(c * CORES, CORES), :, :head_dim].reshape(chunk, head_dim)
        values = kv[g, pl.ds(c * CORES, CORES), :, head_dim:].reshape(chunk, head_dim)
        extended = jnp.concatenate([values, jnp.ones_like(values)], axis=1)
        asked = queries[s, pl.ds(g * heads, heads)].reshape(heads * tokens, head_dim)
        found = lax.dot_general(
            asked, keys, (((1,), (1,)), ((), ())), preferred_element_type=jnp.float32
        )
        weights, factors = [], []
        rows = [slice(h * tokens, (h + 1) * tokens) for h in range(heads)]
        for r in rows:
            masked = found[r] * scale + bias[s, c]
            largest = jnp.max(jnp.maximum(masked[:, :tokens], masked[:, tokens:]), axis=1, keepdims=True)
            before = top[s, g, r, :]
            highest = jnp.maximum(before, largest)
            top[s, g, r, :] = highest
            factors.append(jnp.exp2(before - highest))
            weights.append(
                jnp.exp2(masked - jnp.concatenate([highest] * CORES, axis=1)).astype(jnp.bfloat16)
            )
        added = jnp.dot(jnp.concatenate(weights, axis=0), extended, preferred_element_type=jnp.float32)
        for r, factor in zip(rows, factors):
            acc[s, g, r, :] = acc[s, g, r, :] * jnp.concatenate([factor] * CORES, axis=1) + added[r]

    def over_steps(g, c):
        def body(s, _):
            attend(s, g, c)
            return 0

        lax.fori_loop(0, steps, body, 0)

    for g in range(groups):
        twin_arrival(g, 0).wait_recv()

    def hop_body(hop, _):
        c = pair - hop
        for g in range(groups):
            over_steps(g, c)
            if g == 0:
                @pl.when(hop < pair)
                def _():
                    for each in range(groups):
                        direct_arrival(each, hop + 1).wait_recv()
                        twin_copy(each, hop + 1).start()

        @pl.when(hop < pair)
        def _():
            for each in range(groups):
                twin_arrival(each, hop + 1).wait_recv()

        return 0

    lax.fori_loop(0, pair + 1, hop_body, 0)

    def finish(i, _):
        s, h = i // local_heads, i % local_heads
        g = h // heads
        part = pl.ds(pl.multiple_of(h % heads * tokens, tokens), tokens)
        out_ref[s, h] = (acc[s, g, part, :head_dim] / acc[s, g, part, head_dim:]).astype(out_ref.dtype)
        return 0

    lax.fori_loop(0, steps * local_heads, finish, 0)

    for g in range(groups):
        for k in range(1, sections):
            part_copy(g, k).wait_send()

        def sent(d, _):
            direct_copy(g, d).wait_send()
            return 0

        def passed(hop, _):
            twin_copy(g, hop).wait_send()
            return 0

        lax.fori_loop(1, pairs - pair, sent, 0)
        lax.fori_loop(0, pair + 1, passed, 0)


def per_device(sections, shards, features, norm_gain, kv_weight, queries, step_kv, doc_ids, block_lists):
    steps, local_heads, tokens, head_dim = queries.shape
    groups = step_kv.shape[1]
    rows = local_heads // groups * tokens
    width = 2 * head_dim
    local_width = features.shape[1]
    blocks = block_lists.shape[1]
    block_len = doc_ids.shape[0] // blocks
    pairs = shards // CORES
    others = sections - 1
    dma = pltpu.SemaphoreType.DMA
    vmem = pl.BlockSpec(memory_space=pltpu.VMEM)
    anywhere = pl.BlockSpec(memory_space=pl.ANY)
    return pl.pallas_call(
        functools.partial(fused_kernel, sections, shards, local_width * sections, block_len),
        out_shape=(
            jax.ShapeDtypeStruct(queries.shape, jnp.bfloat16),
            jax.ShapeDtypeStruct((groups, tokens, width), jnp.bfloat16),
        ),
        in_specs=[anywhere] * 5 + [vmem, pl.BlockSpec(memory_space=pltpu.SMEM)],
        out_specs=(vmem, vmem),
        scratch_shapes=[
            pltpu.VMEM((tokens, local_width), jnp.bfloat16),
            pltpu.VMEM((1, local_width), jnp.float32),
            pltpu.VMEM(queries.shape, jnp.bfloat16),
            pltpu.VMEM(step_kv.shape, jnp.bfloat16),
            pltpu.VMEM((groups * sections, local_width, width), jnp.bfloat16),
            pltpu.VMEM((tokens, local_width), jnp.bfloat16),
            pltpu.VMEM((groups, tokens, width), jnp.float32),
            pltpu.VMEM((groups, others, tokens, width), jnp.bfloat16),
            pltpu.VMEM((groups, others, tokens, width), jnp.bfloat16),
            pltpu.VMEM((8, tokens), jnp.float32),
            pltpu.VMEM((others, 8, tokens), jnp.float32),
            pltpu.VMEM((groups, shards, tokens, width), jnp.bfloat16),
            pltpu.VMEM((steps, pairs, tokens, CORES * tokens), jnp.float32),
            pltpu.VMEM((steps, groups, rows, tokens), jnp.float32),
            pltpu.VMEM((steps, groups, rows, width), jnp.float32),
            dma((4,)),
            dma((groups * sections,)),
            dma((groups, others)),
            dma((groups, others)),
            dma((others,)),
            dma((others,)),
            dma((groups, pairs)),
            dma((groups, pairs)),
            dma((groups, pairs)),
            dma((groups, pairs)),
        ],
        compiler_params=pltpu.CompilerParams(
            collective_id=0, has_side_effects=True, vmem_limit_bytes=60 * 1024 * 1024
        ),
    )(
        features,
        norm_gain.reshape(1, local_width),
        kv_weight,
        queries,
        step_kv,
        doc_ids.reshape(shards, tokens),
        block_lists,
    )


def solution(mesh):
    in_specs = (
        P("seq", "section"),
        P("section"),
        P("section", None),
        P(None, "section", "seq", None),
        P(None, "section", "seq", None),
        P(),
        P(),
    )
    out_specs = (P(None, "section", "seq", None), P("section", "seq", None))
    body = functools.partial(per_device, mesh.shape["section"], mesh.shape["seq"])
    return jax.shard_map(body, mesh=mesh, in_specs=in_specs, out_specs=out_specs, check_vma=False)
```

```python
import functools
import math

import jax
import jax.numpy as jnp
from jax import lax
from jax.experimental import pallas as pl
from jax.experimental.pallas import tpu as pltpu
from jax.sharding import PartitionSpec as P

neg_fill = -1e30
MESH = pl.DeviceIdType.MESH
CORES = 2


def flipped(index, mask, count):
    result, bit = 0, 1
    while bit < count:
        own = (index // bit) % 2
        result = result + bit * ((1 - own) if mask & bit else own)
        bit *= 2
    return result


def fused_kernel(
    sections, shards, feature_width, block_len,
    feat_ref, gain_ref, weight_ref, query_ref, step_ref, docs_ref, list_smem,
    out_ref, cache_ref,
    features, gain, queries, step_kv, weight_buf, scaled, own_part, send_buf, recv_buf,
    square_send, square_recv, kv, bias, top, acc,
    load_sem, weight_sem, rs_send, rs_recv, sq_send, sq_recv,
    direct_send, direct_recv, twin_send, twin_recv,
):
    section = lax.axis_index("section")
    shard = lax.axis_index("seq")
    groups, _, tokens, width = kv.shape
    steps, local_heads, _, head_dim = queries.shape
    heads = local_heads // groups
    entries = list_smem.shape[2]
    chunk = CORES * tokens
    pairs = shards // CORES
    pair, core = shard // CORES, shard % CORES
    twin = pair * CORES + 1 - core
    scale = math.log2(math.e) / math.sqrt(head_dim)
    order = list(range(sections - 1, -1, -1))
    span = groups * width
    row_blocks = tokens // block_len

    def weight_copy(slot):
        column = pl.multiple_of(flipped(section, order[slot], sections) * span, span)
        return pltpu.make_async_copy(
            weight_ref.at[:, pl.ds(column, span)], weight_buf.at[slot], weight_sem.at[slot]
        )

    feature_load = pltpu.make_async_copy(feat_ref, features, load_sem.at[0])
    gain_load = pltpu.make_async_copy(gain_ref, gain, load_sem.at[1])
    step_load = pltpu.make_async_copy(step_ref, step_kv, load_sem.at[2])
    query_load = pltpu.make_async_copy(query_ref, queries, load_sem.at[3])
    for load in (feature_load, gain_load, step_load, query_load):
        load.start()
    for slot in range(len(order)):
        weight_copy(slot).start()

    barrier = pltpu.get_barrier_semaphore()
    for k in range(1, sections):
        pl.semaphore_signal(
            barrier, inc=1, device_id={"section": flipped(section, k, sections)}, device_id_type=MESH
        )
    pl.semaphore_signal(barrier, inc=1, device_id={"seq": twin}, device_id_type=MESH)
    for d in range(1, pairs):
        other = (pair + d) % pairs * CORES + core
        pl.semaphore_signal(barrier, inc=1, device_id={"seq": other}, device_id_type=MESH)

    feature_load.wait()
    gain_load.wait()
    floated = features[...].astype(jnp.float32)
    squares = jnp.sum(floated * floated, axis=1, keepdims=True)
    square_rows = jnp.transpose(jnp.broadcast_to(squares, (tokens, tokens)))[:8]
    square_send[...] = square_rows

    pl.semaphore_wait(barrier, sections + pairs - 1)

    def square_copy(k):
        return pltpu.make_async_remote_copy(
            src_ref=square_send, dst_ref=square_recv.at[k - 1],
            send_sem=sq_send.at[k - 1], recv_sem=sq_recv.at[k - 1],
            device_id={"section": flipped(section, k, sections)}, device_id_type=MESH,
        )

    def part_copy(g, k):
        return pltpu.make_async_remote_copy(
            src_ref=send_buf.at[g, k - 1], dst_ref=recv_buf.at[g, k - 1],
            send_sem=rs_send.at[g, k - 1], recv_sem=rs_recv.at[g, k - 1],
            device_id={"section": flipped(section, k, sections)}, device_id_type=MESH,
        )

    def direct_copy(g, d):
        place = kv.at[g, shard]
        return pltpu.make_async_remote_copy(
            src_ref=place, dst_ref=place,
            send_sem=direct_send.at[g, d], recv_sem=direct_recv.at[g, d],
            device_id={"seq": shard + CORES * d}, device_id_type=MESH,
        )

    def direct_arrival(g, d):
        place = kv.at[g, shard - CORES * d]
        return pltpu.make_async_remote_copy(
            src_ref=place, dst_ref=place,
            send_sem=direct_send.at[g, d], recv_sem=direct_recv.at[g, d],
            device_id={"seq": twin}, device_id_type=MESH,
        )

    def twin_copy(g, hop):
        place = kv.at[g, shard - CORES * hop]
        return pltpu.make_async_remote_copy(
            src_ref=place, dst_ref=place,
            send_sem=twin_send.at[g, hop], recv_sem=twin_recv.at[g, hop],
            device_id={"seq": twin}, device_id_type=MESH,
        )

    def twin_arrival(g, hop):
        place = kv.at[g, twin - CORES * hop]
        return pltpu.make_async_remote_copy(
            src_ref=place, dst_ref=place,
            send_sem=twin_send.at[g, hop], recv_sem=twin_recv.at[g, hop],
            device_id={"seq": twin}, device_id_type=MESH,
        )

    def own_steps(h, _):
        g = h // heads
        part = pl.ds(pl.multiple_of(h % heads * tokens, tokens), tokens)
        keys = [step_kv[m, g, :, :head_dim].astype(jnp.float32) for m in range(steps)]
        values = [step_kv[m, g, :, head_dim:].astype(jnp.float32) for m in range(steps)]
        for s in range(steps):
            query = queries[s, h].astype(jnp.float32)
            found = [jnp.sum(query * keys[m], axis=1, keepdims=True) * scale for m in range(s + 1)]
            highest = functools.reduce(jnp.maximum, found)
            weights = [jnp.exp2(one - highest) for one in found]
            rounded = [w.astype(jnp.bfloat16).astype(jnp.float32) for w in weights]
            top[s, g, part, :] = jnp.broadcast_to(highest, (tokens, tokens))
            acc[s, g, part, :head_dim] = sum(w * values[m] for m, w in enumerate(rounded))
            acc[s, g, part, head_dim:] = jnp.broadcast_to(sum(weights), (tokens, head_dim))
        return 0

    def fill_bias(c, _):
        row = lax.broadcasted_iota(jnp.int32, (tokens, tokens), 0)
        column = lax.broadcasted_iota(jnp.int32, (tokens, tokens), 1)
        lane = lax.broadcasted_iota(jnp.int32, (1, tokens), 1)
        own_docs = docs_ref[pl.ds(shard, 1), :].astype(jnp.float32)
        row_docs = jnp.transpose(jnp.broadcast_to(own_docs, (tokens, tokens)))
        for half in range(CORES):
            key_shard = c * CORES + half
            key_block = key_shard * row_blocks + lane // block_len
            key_docs = docs_ref[pl.ds(key_shard, 1), :].astype(jnp.float32)
            shared = (row_docs == key_docs) & (key_shard * tokens + column <= shard * tokens + row)
            for s in range(steps):
                listed = []
                for r in range(row_blocks):
                    marks = jnp.full((1, tokens), neg_fill, jnp.float32)
                    for e in range(entries):
                        entry = list_smem[s, shard * row_blocks + r, e]
                        marks = jnp.where(key_block == entry, 0.0, marks)
                    listed.append(marks)
                marks = jnp.broadcast_to(listed[-1], (tokens, tokens))
                for r in range(row_blocks - 2, -1, -1):
                    marks = jnp.where(row < (r + 1) * block_len, listed[r], marks)
                bias[s, c, :, half * tokens:(half + 1) * tokens] = jnp.where(shared, marks, neg_fill)
        return 0

    for k in range(1, sections):
        square_copy(k).start()

    step_load.wait()
    query_load.wait()
    lax.fori_loop(0, local_heads // 4, own_steps, 0)

    total = square_rows
    for k in range(1, sections):
        square_copy(k).wait()
        total = total + square_recv[k - 1]
    mean = jnp.transpose(jnp.broadcast_to(total[:1], (tokens, tokens))) / feature_width
    inverse = lax.rsqrt(mean + 1e-05)
    for first in range(0, features.shape[1], tokens):
        part = pl.ds(first, tokens)
        scaled[:, part] = (
            features[:, part].astype(jnp.float32) * inverse * gain[:, part]
        ).astype(jnp.bfloat16)

    for slot, k in enumerate(order):
        weight_copy(slot).wait()
        part = jnp.dot(scaled[...], weight_buf[slot], preferred_element_type=jnp.float32)
        for g in range(groups):
            columns = part[:, g * width:(g + 1) * width]
            if k:
                send_buf[g, k - 1] = columns.astype(jnp.bfloat16)
                part_copy(g, k).start()
            else:
                own_part[g] = columns

    lax.fori_loop(0, pair + 1, fill_bias, 0)
    lax.fori_loop(local_heads // 4, local_heads // 2, own_steps, 0)

    for g in range(groups):
        summed = own_part[g]
        for k in range(sections - 1, 0, -1):
            part_copy(g, k).wait_recv()
            summed = summed + recv_buf[g, k - 1].astype(jnp.float32)
        rounded = summed.astype(jnp.bfloat16)
        kv[g, shard] = rounded
        cache_ref[g] = rounded
        twin_copy(g, 0).start()

        @pl.when(pair < pairs - 1)
        def _():
            direct_copy(g, 1).start()

    def send(d, _):
        for g in range(groups):
            direct_copy(g, d).start()
        return 0

    lax.fori_loop(2, pairs - pair, send, 0)
    lax.fori_loop(local_heads // 2, local_heads, own_steps, 0)

    def attend(s, g, c):
        keys = kv[g, pl.ds(c * CORES, CORES), :, :head_dim].reshape(chunk, head_dim)
        values = kv[g, pl.ds(c * CORES, CORES), :, head_dim:].reshape(chunk, head_dim)
        extended = jnp.concatenate([values, jnp.ones_like(values)], axis=1)
        asked = queries[s, pl.ds(g * heads, heads)].reshape(heads * tokens, head_dim)
        found = lax.dot_general(
            asked, keys, (((1,), (1,)), ((), ())), preferred_element_type=jnp.float32
        )
        weights, factors = [], []
        rows = [slice(h * tokens, (h + 1) * tokens) for h in range(heads)]
        for r in rows:
            masked = found[r] * scale + bias[s, c]
            largest = jnp.max(jnp.maximum(masked[:, :tokens], masked[:, tokens:]), axis=1, keepdims=True)
            before = top[s, g, r, :]
            highest = jnp.maximum(before, largest)
            top[s, g, r, :] = highest
            factors.append(jnp.exp2(before - highest))
            weights.append(
                jnp.exp2(masked - jnp.concatenate([highest] * CORES, axis=1)).astype(jnp.bfloat16)
            )
        added = jnp.dot(jnp.concatenate(weights, axis=0), extended, preferred_element_type=jnp.float32)
        for r, factor in zip(rows, factors):
            acc[s, g, r, :] = acc[s, g, r, :] * jnp.concatenate([factor] * CORES, axis=1) + added[r]

    def over_steps(g, c):
        def body(s, _):
            attend(s, g, c)
            return 0

        lax.fori_loop(0, steps, body, 0)

    for g in range(groups):
        twin_arrival(g, 0).wait_recv()

    def hop_body(hop, _):
        c = pair - hop
        for g in range(groups):
            over_steps(g, c)
            if g == 0:
                @pl.when(hop < pair)
                def _():
                    for each in range(groups):
                        direct_arrival(each, hop + 1).wait_recv()
                        twin_copy(each, hop + 1).start()

        @pl.when(hop < pair)
        def _():
            for each in range(groups):
                twin_arrival(each, hop + 1).wait_recv()

        return 0

    lax.fori_loop(0, pair + 1, hop_body, 0)

    def finish(i, _):
        s, h = i // local_heads, i % local_heads
        g = h // heads
        part = pl.ds(pl.multiple_of(h % heads * tokens, tokens), tokens)
        out_ref[s, h] = (acc[s, g, part, :head_dim] / acc[s, g, part, head_dim:]).astype(out_ref.dtype)
        return 0

    lax.fori_loop(0, steps * local_heads, finish, 0)

    for g in range(groups):
        for k in range(1, sections):
            part_copy(g, k).wait_send()

        def sent(d, _):
            direct_copy(g, d).wait_send()
            return 0

        def passed(hop, _):
            twin_copy(g, hop).wait_send()
            return 0

        lax.fori_loop(1, pairs - pair, sent, 0)
        lax.fori_loop(0, pair + 1, passed, 0)


def deliver_kernel(attended, cache, attended_out, cache_out, buf, cache_buf, load_sem, store_sem):
    steps = attended.shape[0]
    parts = [(attended.at[s], buf.at[s], attended_out.at[s]) for s in range(steps)]
    parts.append((cache, cache_buf, cache_out))
    loads = [pltpu.make_async_copy(p[0], p[1], load_sem.at[i]) for i, p in enumerate(parts)]
    stores = [pltpu.make_async_copy(p[1], p[2], store_sem.at[i]) for i, p in enumerate(parts)]
    for load in loads:
        load.start()
    for load, store in zip(loads, stores):
        load.wait()
        store.start()
    for store in stores:
        store.wait()


def per_device(sections, shards, features, norm_gain, kv_weight, queries, step_kv, doc_ids, block_lists):
    steps, local_heads, tokens, head_dim = queries.shape
    groups = step_kv.shape[1]
    rows = local_heads // groups * tokens
    width = 2 * head_dim
    local_width = features.shape[1]
    blocks = block_lists.shape[1]
    block_len = doc_ids.shape[0] // blocks
    pairs = shards // CORES
    others = sections - 1
    dma = pltpu.SemaphoreType.DMA
    vmem = pl.BlockSpec(memory_space=pltpu.VMEM)
    anywhere = pl.BlockSpec(memory_space=pl.ANY)
    results = pl.pallas_call(
        functools.partial(fused_kernel, sections, shards, local_width * sections, block_len),
        out_shape=(
            jax.ShapeDtypeStruct(queries.shape, jnp.bfloat16),
            jax.ShapeDtypeStruct((groups, tokens, width), jnp.bfloat16),
        ),
        in_specs=[anywhere] * 5 + [vmem, pl.BlockSpec(memory_space=pltpu.SMEM)],
        out_specs=(vmem, vmem),
        scratch_shapes=[
            pltpu.VMEM((tokens, local_width), jnp.bfloat16),
            pltpu.VMEM((1, local_width), jnp.float32),
            pltpu.VMEM(queries.shape, jnp.bfloat16),
            pltpu.VMEM(step_kv.shape, jnp.bfloat16),
            pltpu.VMEM((sections, local_width, groups * width), jnp.bfloat16),
            pltpu.VMEM((tokens, local_width), jnp.bfloat16),
            pltpu.VMEM((groups, tokens, width), jnp.float32),
            pltpu.VMEM((groups, others, tokens, width), jnp.bfloat16),
            pltpu.VMEM((groups, others, tokens, width), jnp.bfloat16),
            pltpu.VMEM((8, tokens), jnp.float32),
            pltpu.VMEM((others, 8, tokens), jnp.float32),
            pltpu.VMEM((groups, shards, tokens, width), jnp.bfloat16),
            pltpu.VMEM((steps, pairs, tokens, CORES * tokens), jnp.float32),
            pltpu.VMEM((steps, groups, rows, tokens), jnp.float32),
            pltpu.VMEM((steps, groups, rows, width), jnp.float32),
            dma((4,)),
            dma((sections,)),
            dma((groups, others)),
            dma((groups, others)),
            dma((others,)),
            dma((others,)),
            dma((groups, pairs)),
            dma((groups, pairs)),
            dma((groups, pairs)),
            dma((groups, pairs)),
        ],
        compiler_params=pltpu.CompilerParams(
            collective_id=0, has_side_effects=True, vmem_limit_bytes=60 * 1024 * 1024
        ),
    )(
        features,
        norm_gain.reshape(1, local_width),
        kv_weight,
        queries,
        step_kv,
        doc_ids.reshape(shards, tokens),
        block_lists,
    )
    return pl.pallas_call(
        deliver_kernel,
        out_shape=tuple(jax.ShapeDtypeStruct(r.shape, r.dtype) for r in results),
        in_specs=[anywhere] * 2,
        out_specs=(anywhere, anywhere),
        scratch_shapes=[
            *(pltpu.VMEM(r.shape, r.dtype) for r in results), dma((steps + 1,)), dma((steps + 1,))
        ],
        compiler_params=pltpu.CompilerParams(vmem_limit_bytes=60 * 1024 * 1024),
    )(*results)


def solution(mesh):
    in_specs = (
        P("seq", "section"),
        P("section"),
        P("section", None),
        P(None, "section", "seq", None),
        P(None, "section", "seq", None),
        P(),
        P(),
    )
    out_specs = (P(None, "section", "seq", None), P("section", "seq", None))
    body = functools.partial(per_device, mesh.shape["section"], mesh.shape["seq"])
    return jax.shard_map(body, mesh=mesh, in_specs=in_specs, out_specs=out_specs, check_vma=False)
```

```python
import functools
import math

import jax
import jax.numpy as jnp
from jax import lax
from jax.experimental import pallas as pl
from jax.experimental.pallas import tpu as pltpu
from jax.sharding import PartitionSpec as P

neg_fill = -1e30
MESH = pl.DeviceIdType.MESH
CORES = 2


def flipped(index, mask, count):
    result, bit = 0, 1
    while bit < count:
        own = (index // bit) % 2
        result = result + bit * ((1 - own) if mask & bit else own)
        bit *= 2
    return result


def fused_kernel(
    sections, shards, feature_width, block_len,
    feat_ref, gain_ref, weight_ref, query_ref, step_ref, docs_ref, list_smem,
    out_ref, cache_ref,
    features, gain, queries, step_kv, weight_buf, scaled, own_part, send_buf, recv_buf,
    square_send, square_recv, kv, bias, top, acc,
    load_sem, weight_sem, rs_send, rs_recv, sq_send, sq_recv,
    chain_send, chain_recv, twin_send, twin_recv,
):
    section = lax.axis_index("section")
    shard = lax.axis_index("seq")
    groups, _, tokens, width = kv.shape
    steps, local_heads, _, head_dim = queries.shape
    heads = local_heads // groups
    entries = list_smem.shape[2]
    chunk = CORES * tokens
    pairs = shards // CORES
    pair = shard // CORES
    twin = pair * CORES + 1 - shard % CORES
    scale = math.log2(math.e) / math.sqrt(head_dim)
    order = list(range(sections - 1, -1, -1))
    span = groups * width
    row_blocks = tokens // block_len

    def weight_copy(slot):
        column = pl.multiple_of(flipped(section, order[slot], sections) * span, span)
        return pltpu.make_async_copy(
            weight_ref.at[:, pl.ds(column, span)], weight_buf.at[slot], weight_sem.at[slot]
        )

    feature_load = pltpu.make_async_copy(feat_ref, features, load_sem.at[0])
    gain_load = pltpu.make_async_copy(gain_ref, gain, load_sem.at[1])
    step_load = pltpu.make_async_copy(step_ref, step_kv, load_sem.at[2])
    query_load = pltpu.make_async_copy(query_ref, queries, load_sem.at[3])
    for load in (feature_load, gain_load, step_load, query_load):
        load.start()
    for slot in range(len(order)):
        weight_copy(slot).start()

    barrier = pltpu.get_barrier_semaphore()
    for k in range(1, sections):
        pl.semaphore_signal(
            barrier, inc=1, device_id={"section": flipped(section, k, sections)}, device_id_type=MESH
        )
    pl.semaphore_signal(barrier, inc=1, device_id={"seq": twin}, device_id_type=MESH)

    @pl.when(pair < pairs - 1)
    def _():
        pl.semaphore_signal(barrier, inc=1, device_id={"seq": shard + CORES}, device_id_type=MESH)

    @pl.when(pair > 0)
    def _():
        pl.semaphore_signal(barrier, inc=1, device_id={"seq": shard - CORES}, device_id_type=MESH)

    feature_load.wait()
    gain_load.wait()
    floated = features[...].astype(jnp.float32)
    squares = jnp.sum(floated * floated, axis=1, keepdims=True)
    square_rows = jnp.transpose(jnp.broadcast_to(squares, (tokens, tokens)))[:8]
    square_send[...] = square_rows

    pl.semaphore_wait(barrier, sections + jnp.where(pair > 0, 1, 0) + jnp.where(pair < pairs - 1, 1, 0))

    def square_copy(k):
        return pltpu.make_async_remote_copy(
            src_ref=square_send, dst_ref=square_recv.at[k - 1],
            send_sem=sq_send.at[k - 1], recv_sem=sq_recv.at[k - 1],
            device_id={"section": flipped(section, k, sections)}, device_id_type=MESH,
        )

    def part_copy(g, k):
        return pltpu.make_async_remote_copy(
            src_ref=send_buf.at[g, k - 1], dst_ref=recv_buf.at[g, k - 1],
            send_sem=rs_send.at[g, k - 1], recv_sem=rs_recv.at[g, k - 1],
            device_id={"section": flipped(section, k, sections)}, device_id_type=MESH,
        )

    def chain_copy(g, hop):
        place = kv.at[g, shard - CORES * hop]
        return pltpu.make_async_remote_copy(
            src_ref=place, dst_ref=place,
            send_sem=chain_send.at[g, hop], recv_sem=chain_recv.at[g, hop + 1],
            device_id={"seq": shard + CORES}, device_id_type=MESH,
        )

    def chain_arrival(g, hop):
        place = kv.at[g, shard - CORES * hop]
        return pltpu.make_async_remote_copy(
            src_ref=place, dst_ref=place,
            send_sem=chain_send.at[g, hop], recv_sem=chain_recv.at[g, hop],
            device_id={"seq": twin}, device_id_type=MESH,
        )

    def twin_copy(g, hop):
        place = kv.at[g, shard - CORES * hop]
        return pltpu.make_async_remote_copy(
            src_ref=place, dst_ref=place,
            send_sem=twin_send.at[g, hop], recv_sem=twin_recv.at[g, hop],
            device_id={"seq": twin}, device_id_type=MESH,
        )

    def twin_arrival(g, hop):
        place = kv.at[g, twin - CORES * hop]
        return pltpu.make_async_remote_copy(
            src_ref=place, dst_ref=place,
            send_sem=twin_send.at[g, hop], recv_sem=twin_recv.at[g, hop],
            device_id={"seq": twin}, device_id_type=MESH,
        )

    def own_steps(h, _):
        g = h // heads
        part = pl.ds(pl.multiple_of(h % heads * tokens, tokens), tokens)
        keys = [step_kv[m, g, :, :head_dim].astype(jnp.float32) for m in range(steps)]
        values = [step_kv[m, g, :, head_dim:].astype(jnp.float32) for m in range(steps)]
        for s in range(steps):
            query = queries[s, h].astype(jnp.float32)
            found = [jnp.sum(query * keys[m], axis=1, keepdims=True) * scale for m in range(s + 1)]
            highest = functools.reduce(jnp.maximum, found)
            weights = [jnp.exp2(one - highest) for one in found]
            rounded = [w.astype(jnp.bfloat16).astype(jnp.float32) for w in weights]
            top[s, g, part, :] = jnp.broadcast_to(highest, (tokens, tokens))
            acc[s, g, part, :head_dim] = sum(w * values[m] for m, w in enumerate(rounded))
            acc[s, g, part, head_dim:] = jnp.broadcast_to(sum(weights), (tokens, head_dim))
        return 0

    def fill_bias(c, _):
        row = lax.broadcasted_iota(jnp.int32, (tokens, tokens), 0)
        column = lax.broadcasted_iota(jnp.int32, (tokens, tokens), 1)
        lane = lax.broadcasted_iota(jnp.int32, (1, tokens), 1)
        own_docs = docs_ref[pl.ds(shard, 1), :].astype(jnp.float32)
        row_docs = jnp.transpose(jnp.broadcast_to(own_docs, (tokens, tokens)))
        for half in range(CORES):
            key_shard = c * CORES + half
            key_block = key_shard * row_blocks + lane // block_len
            key_docs = docs_ref[pl.ds(key_shard, 1), :].astype(jnp.float32)
            shared = (row_docs == key_docs) & (key_shard * tokens + column <= shard * tokens + row)
            for s in range(steps):
                listed = []
                for r in range(row_blocks):
                    marks = jnp.full((1, tokens), neg_fill, jnp.float32)
                    for e in range(entries):
                        entry = list_smem[s, shard * row_blocks + r, e]
                        marks = jnp.where(key_block == entry, 0.0, marks)
                    listed.append(marks)
                marks = jnp.broadcast_to(listed[-1], (tokens, tokens))
                for r in range(row_blocks - 2, -1, -1):
                    marks = jnp.where(row < (r + 1) * block_len, listed[r], marks)
                bias[s, c, :, half * tokens:(half + 1) * tokens] = jnp.where(shared, marks, neg_fill)
        return 0

    for k in range(1, sections):
        square_copy(k).start()

    step_load.wait()
    query_load.wait()
    lax.fori_loop(0, local_heads // 4, own_steps, 0)

    total = square_rows
    for k in range(1, sections):
        square_copy(k).wait()
        total = total + square_recv[k - 1]
    mean = jnp.transpose(jnp.broadcast_to(total[:1], (tokens, tokens))) / feature_width
    inverse = lax.rsqrt(mean + 1e-05)
    for first in range(0, features.shape[1], tokens):
        part = pl.ds(first, tokens)
        scaled[:, part] = (
            features[:, part].astype(jnp.float32) * inverse * gain[:, part]
        ).astype(jnp.bfloat16)

    for slot, k in enumerate(order):
        weight_copy(slot).wait()
        part = jnp.dot(scaled[...], weight_buf[slot], preferred_element_type=jnp.float32)
        for g in range(groups):
            columns = part[:, g * width:(g + 1) * width]
            if k:
                send_buf[g, k - 1] = columns.astype(jnp.bfloat16)
                part_copy(g, k).start()
            else:
                own_part[g] = columns

    lax.fori_loop(0, pair + 1, fill_bias, 0)
    lax.fori_loop(local_heads // 4, local_heads // 2, own_steps, 0)

    for g in range(groups):
        summed = own_part[g]
        for k in range(sections - 1, 0, -1):
            part_copy(g, k).wait_recv()
            summed = summed + recv_buf[g, k - 1].astype(jnp.float32)
        rounded = summed.astype(jnp.bfloat16)
        kv[g, shard] = rounded
        cache_ref[g] = rounded
        twin_copy(g, 0).start()

        @pl.when(pair < pairs - 1)
        def _():
            chain_copy(g, 0).start()

    lax.fori_loop(local_heads // 2, local_heads, own_steps, 0)

    def attend(s, g, c):
        keys = kv[g, pl.ds(c * CORES, CORES), :, :head_dim].reshape(chunk, head_dim)
        values = kv[g, pl.ds(c * CORES, CORES), :, head_dim:].reshape(chunk, head_dim)
        extended = jnp.concatenate([values, jnp.ones_like(values)], axis=1)
        asked = queries[s, pl.ds(g * heads, heads)].reshape(heads * tokens, head_dim)
        found = lax.dot_general(
            asked, keys, (((1,), (1,)), ((), ())), preferred_element_type=jnp.float32
        )
        weights, factors = [], []
        rows = [slice(h * tokens, (h + 1) * tokens) for h in range(heads)]
        for r in rows:
            masked = found[r] * scale + bias[s, c]
            largest = jnp.max(jnp.maximum(masked[:, :tokens], masked[:, tokens:]), axis=1, keepdims=True)
            before = top[s, g, r, :]
            highest = jnp.maximum(before, largest)
            top[s, g, r, :] = highest
            factors.append(jnp.exp2(before - highest))
            weights.append(
                jnp.exp2(masked - jnp.concatenate([highest] * CORES, axis=1)).astype(jnp.bfloat16)
            )
        added = jnp.dot(jnp.concatenate(weights, axis=0), extended, preferred_element_type=jnp.float32)
        for r, factor in zip(rows, factors):
            acc[s, g, r, :] = acc[s, g, r, :] * jnp.concatenate([factor] * CORES, axis=1) + added[r]

    def over_steps(g, c):
        def body(s, _):
            attend(s, g, c)
            return 0

        lax.fori_loop(0, steps, body, 0)

    def pass_on(hop):
        for g in range(groups):
            chain_arrival(g, hop).wait_recv()

            @pl.when(pair < pairs - 1)
            def _():
                chain_copy(g, hop).start()

            twin_copy(g, hop).start()

    for g in range(groups):
        twin_arrival(g, 0).wait_recv()

    @pl.when(pair > 0)
    def _():
        pass_on(1)

    def hop_body(hop, _):
        for g in range(groups):
            over_steps(g, pair - hop)

        @pl.when(hop + 2 <= pair)
        def _():
            pass_on(hop + 2)

        @pl.when(hop < pair)
        def _():
            for g in range(groups):
                twin_arrival(g, hop + 1).wait_recv()

        return 0

    lax.fori_loop(0, pair + 1, hop_body, 0)

    def finish(i, _):
        s, h = i // local_heads, i % local_heads
        g = h // heads
        part = pl.ds(pl.multiple_of(h % heads * tokens, tokens), tokens)
        out_ref[s, h] = (acc[s, g, part, :head_dim] / acc[s, g, part, head_dim:]).astype(out_ref.dtype)
        return 0

    lax.fori_loop(0, steps * local_heads, finish, 0)

    for g in range(groups):
        for k in range(1, sections):
            part_copy(g, k).wait_send()

        def passed(hop, _):
            twin_copy(g, hop).wait_send()

            @pl.when(pair < pairs - 1)
            def _():
                chain_copy(g, hop).wait_send()

            return 0

        lax.fori_loop(0, pair + 1, passed, 0)


def deliver_kernel(attended, cache, attended_out, cache_out, buf, cache_buf, load_sem, store_sem):
    steps = attended.shape[0]
    parts = [(attended.at[s], buf.at[s], attended_out.at[s]) for s in range(steps)]
    parts.append((cache, cache_buf, cache_out))
    loads = [pltpu.make_async_copy(p[0], p[1], load_sem.at[i]) for i, p in enumerate(parts)]
    stores = [pltpu.make_async_copy(p[1], p[2], store_sem.at[i]) for i, p in enumerate(parts)]
    for load in loads:
        load.start()
    for load, store in zip(loads, stores):
        load.wait()
        store.start()
    for store in stores:
        store.wait()


def per_device(sections, shards, features, norm_gain, kv_weight, queries, step_kv, doc_ids, block_lists):
    steps, local_heads, tokens, head_dim = queries.shape
    groups = step_kv.shape[1]
    rows = local_heads // groups * tokens
    width = 2 * head_dim
    local_width = features.shape[1]
    blocks = block_lists.shape[1]
    block_len = doc_ids.shape[0] // blocks
    pairs = shards // CORES
    others = sections - 1
    dma = pltpu.SemaphoreType.DMA
    vmem = pl.BlockSpec(memory_space=pltpu.VMEM)
    anywhere = pl.BlockSpec(memory_space=pl.ANY)
    results = pl.pallas_call(
        functools.partial(fused_kernel, sections, shards, local_width * sections, block_len),
        out_shape=(
            jax.ShapeDtypeStruct(queries.shape, jnp.bfloat16),
            jax.ShapeDtypeStruct((groups, tokens, width), jnp.bfloat16),
        ),
        in_specs=[anywhere] * 5 + [vmem, pl.BlockSpec(memory_space=pltpu.SMEM)],
        out_specs=(vmem, vmem),
        scratch_shapes=[
            pltpu.VMEM((tokens, local_width), jnp.bfloat16),
            pltpu.VMEM((1, local_width), jnp.float32),
            pltpu.VMEM(queries.shape, jnp.bfloat16),
            pltpu.VMEM(step_kv.shape, jnp.bfloat16),
            pltpu.VMEM((sections, local_width, groups * width), jnp.bfloat16),
            pltpu.VMEM((tokens, local_width), jnp.bfloat16),
            pltpu.VMEM((groups, tokens, width), jnp.float32),
            pltpu.VMEM((groups, others, tokens, width), jnp.bfloat16),
            pltpu.VMEM((groups, others, tokens, width), jnp.bfloat16),
            pltpu.VMEM((8, tokens), jnp.float32),
            pltpu.VMEM((others, 8, tokens), jnp.float32),
            pltpu.VMEM((groups, shards, tokens, width), jnp.bfloat16),
            pltpu.VMEM((steps, pairs, tokens, CORES * tokens), jnp.float32),
            pltpu.VMEM((steps, groups, rows, tokens), jnp.float32),
            pltpu.VMEM((steps, groups, rows, width), jnp.float32),
            dma((4,)),
            dma((sections,)),
            dma((groups, others)),
            dma((groups, others)),
            dma((others,)),
            dma((others,)),
            dma((groups, pairs)),
            dma((groups, pairs)),
            dma((groups, pairs)),
            dma((groups, pairs)),
        ],
        compiler_params=pltpu.CompilerParams(
            collective_id=0, has_side_effects=True, vmem_limit_bytes=60 * 1024 * 1024
        ),
    )(
        features,
        norm_gain.reshape(1, local_width),
        kv_weight,
        queries,
        step_kv,
        doc_ids.reshape(shards, tokens),
        block_lists,
    )
    return pl.pallas_call(
        deliver_kernel,
        out_shape=tuple(jax.ShapeDtypeStruct(r.shape, r.dtype) for r in results),
        in_specs=[anywhere] * 2,
        out_specs=(anywhere, anywhere),
        scratch_shapes=[
            *(pltpu.VMEM(r.shape, r.dtype) for r in results), dma((steps + 1,)), dma((steps + 1,))
        ],
        compiler_params=pltpu.CompilerParams(vmem_limit_bytes=60 * 1024 * 1024),
    )(*results)


def solution(mesh):
    in_specs = (
        P("seq", "section"),
        P("section"),
        P("section", None),
        P(None, "section", "seq", None),
        P(None, "section", "seq", None),
        P(),
        P(),
    )
    out_specs = (P(None, "section", "seq", None), P("section", "seq", None))
    body = functools.partial(per_device, mesh.shape["section"], mesh.shape["seq"])
    return jax.shard_map(body, mesh=mesh, in_specs=in_specs, out_specs=out_specs, check_vma=False)
```
